32 devices in a mesh: groups: 2 (over x), fsdp: 16 (over z, y, core).
Axes of the slice: x: 2, y: 2, z: 4, core: 2. Of those that a mesh axis runs over, the one named last changes fastest.
Arguments:
- layer_input: bfloat16 [12288, 2048], P(('groups', 'fsdp')), parts along dimension 0, may hold values from -6 to 6
- output_gradient: bfloat16 [12288, 6656], P(('groups', 'fsdp')), parts along dimension 0, may hold values from -6 to 6
- frozen_weight: bfloat16 [2048, 6656], P('fsdp'), may hold values from -0.078125 to 0.078125
- adapter_down: bfloat16 [4096, 64], P(('groups', 'fsdp')), parts along dimension 0, may hold values from -0.125 to 0.125
- adapter_up_matrix: bfloat16 [128, 6656], P('groups', 'fsdp'), parts along dimension 0, may hold values from -0.078125 to 0.078125
Outputs:
- grad_input: bfloat16 [12288, 2048], P(('groups', 'fsdp')), parts along dimension 0
- grad_down: float32 [4096, 64], P(('groups', 'fsdp')), parts along dimension 0
- up_matrix_gradient: float32 [128, 6656], P('groups', 'fsdp'), parts along dimension 0
The draws below stay inside these ranges and needn't reach their ends.
There are 2 independent parts, one for each index of `groups`. The reference program is written for one: setup_inputs(seed, part) draws one part's arguments, and reference() takes and returns one part's arrays. A program takes and returns all parts, laid end to end along the dimension named above; an argument that names none is the same for every part. Nothing has to cross between parts.
All inputs are finite; a program needn't handle non-finite values.
Results may differ from the reference program's by a relative error of at most 0.0034.
Values may be sent and summed in bfloat16 or wider, within the bound.
A program may use at most 128 MiB of HBM per device.

```python
import math
import jax
import jax.numpy as jnp

D_TP = 2048
F_TP = 6656
RANK = 64
TOKENS = 6144


def raised(values, own_key, source, target, shards_of, factor):
    def block_of(axis_at):
        return (jnp.arange(values.shape[axis_at]) // (values.shape[axis_at] // shards_of)).reshape((-1,) + (1,) * (values.ndim - 1 - axis_at))

    near = jax.random.permutation(own_key, shards_of)[block_of(target)]
    second = (block_of(target) + shards_of // 2) % shards_of
    return jnp.where((block_of(source) == near) | (block_of(source) == second), factor * values, values)


def levels(key, dims, shards, smallest, high):
    def one(position, shards_of):
        steps = jax.random.uniform(jax.random.fold_in(jax.random.fold_in(key, 6), position), (shards_of,), jnp.float32, smallest / len(shards), high / len(shards))
        return jnp.repeat(jnp.exp(steps), dims[position] // shards_of).reshape((-1,) + (1,) * (len(dims) - position - 1))

    loudness = one(*shards[0])
    for cut in shards[1:]:
        loudness = loudness * one(*cut)
    return loudness


def scatter_about(own_key, dims, spread, bound, shards=(), held_as=jnp.bfloat16):
    drawn = jax.random.normal(own_key, dims, jnp.float32) * spread
    if len(shards) > 0:
        drawn = levels(own_key, dims, shards, -0.22, 0.18) * drawn
    return jnp.clip(drawn, min=-bound, max=bound).astype(held_as)


def gaussian_with(stream_key, dims, width, most, cuts, heavy, kind=jnp.bfloat16):
    values = width * jax.random.normal(stream_key, dims, jnp.float32)
    if cuts:
        values = values * levels(stream_key, dims, cuts, -0.22, 0.18)
    return jnp.clip(raised(values, jax.random.fold_in(stream_key, 3), *heavy), -most, most).astype(kind)


def setup_inputs(seed: int = 0, part: int = 0) -> dict:
    keys = jax.random.split(jax.random.key(seed), 6)
    part_keys = jax.random.split(jax.random.fold_in(keys[5], part), 6)
    return {
        "layer_input": gaussian_with(part_keys[0], (TOKENS, D_TP), 1.0, 6.0, ((0, 16),), (0, 1, 16, 2.0)),
        "output_gradient": gaussian_with(part_keys[1], (TOKENS, F_TP), 1.0, 6.0, ((0, 16),), (0, 1, 16, 2.0)),
        "frozen_weight": scatter_about(keys[2], (D_TP, F_TP), F_TP ** -0.5, 0.078125, ((0, 16),)),
        "adapter_down": scatter_about(part_keys[3], (D_TP, RANK), D_TP ** -0.5, 0.125, ((0, 16),)),
        "adapter_up_matrix": scatter_about(part_keys[4], (RANK, F_TP), F_TP ** -0.5, 0.078125, ((1, 16),)),
    }


adapter_scale = 2.0

def reference(layer_input, output_gradient, frozen_weight, adapter_down, adapter_up_matrix):
    hidden_projection = jnp.dot(layer_input, adapter_down, preferred_element_type=jnp.float32).astype(jnp.bfloat16)
    incoming_gradient = (adapter_scale * jnp.dot(output_gradient, adapter_up_matrix.T, preferred_element_type=jnp.float32)).astype(jnp.bfloat16)
    dense_part = jnp.dot(output_gradient, frozen_weight.T, preferred_element_type=jnp.float32)
    low_rank = jnp.dot(incoming_gradient, adapter_down.T, preferred_element_type=jnp.float32)
    grad_input = (dense_part + low_rank).astype(jnp.bfloat16)
    objective_scale = 1.0 / math.sqrt(TOKENS)
    grad_down = jnp.dot(layer_input.T, incoming_gradient, preferred_element_type=jnp.float32) * objective_scale
    up_matrix_gradient = adapter_scale * jnp.dot(hidden_projection.T, output_gradient, preferred_element_type=jnp.float32) * objective_scale
    return (grad_input, grad_down, up_matrix_gradient)
```

```python
import functools
import math

import jax
import jax.numpy as jnp
from jax import lax
from jax.experimental import pallas as pl
from jax.experimental.pallas import tpu as pltpu
from jax.sharding import PartitionSpec as P

adapter_scale = 2.0
MESH = pl.DeviceIdType.MESH
HALVES = 2


def dot_nt(left, right):
    return lax.dot_general(
        left, right, (((1,), (1,)), ((), ())), preferred_element_type=jnp.float32
    )


def dot_tn(left, right):
    return lax.dot_general(
        left, right, (((0,), (0,)), ((), ())), preferred_element_type=jnp.float32
    )


def chip_at(position, chips, two_columns):
    if not two_columns:
        return position
    return jnp.where(
        position < chips // 2, 2 * position, 2 * (chips - 1 - position) + 1
    )


def place_of(chip, chips, two_columns):
    if not two_columns:
        return chip
    row, column = chip // 2, chip % 2
    return jnp.where(column == 0, row, chips - 1 - row)


def dense_kernel(
    chips, two_columns, rows, features, side, middle,
    grad_ref, weight_ref, upstream_ref, down_ref, out_ref,
    held, grad, local_sem, send_sem, recv_sem, own_send, own_recv,
):
    group, me = lax.axis_index("groups"), lax.axis_index("fsdp")
    core = lax.rem(me, 2)
    place = place_of(me // 2, chips, two_columns)
    role = lax.rem(group, 2)
    steps = chips - 1
    half = rows // HALVES

    def device(position):
        return chip_at(lax.rem(position + 2 * chips, chips), chips, two_columns) * 2 + core

    ahead, behind = (group, device(place + 1)), (group, device(place - 1))
    across = (group + 1 - 2 * role, me)
    sibling = (group, me + 1 - 2 * core)

    load_weight = pltpu.make_async_copy(
        weight_ref, held.at[pl.ds(pl.multiple_of(me * rows, rows), rows)], local_sem.at[0]
    )
    load_grad = pltpu.make_async_copy(grad_ref, grad, local_sem.at[1])
    load_weight.start()
    load_grad.start()

    barrier = pltpu.get_barrier_semaphore()
    for other in (ahead, behind, across, sibling):
        pl.semaphore_signal(barrier, inc=1, device_id=other, device_id_type=MESH)
    pl.semaphore_wait(barrier, 4)

    near = pl.multiple_of(role * (side + middle), 128)
    far = pl.multiple_of((1 - role) * (side + middle), 128)

    def block(owner, h, columns):
        return held.at[pl.ds(pl.multiple_of(owner * rows + h * half, half), half), columns]

    cut_near, cut_far, cut_mid = pl.ds(near, side), pl.ds(far, side), pl.ds(side, middle)

    def copy(kind, h, step, owner, columns, target):
        ref = block(owner, h, columns)
        return pltpu.make_async_remote_copy(
            src_ref=ref, dst_ref=ref,
            send_sem=send_sem.at[kind, h, step], recv_sem=recv_sem.at[kind, h, step],
            device_id=target, device_id_type=MESH,
        )

    def forward(h, step, owner):
        return copy(0, h, step, owner, cut_near, ahead)

    def backward(h, step, owner):
        return copy(1, h, step, owner, cut_mid, behind)

    def cross(h, step, owner):
        return copy(2, h, step, owner, cut_near, across)

    def cross_in(h, step, owner):
        return copy(2, h, step, owner, cut_far, across)

    def share(kind, h, step, owner, columns):
        return copy(3 + kind, h, step, owner, columns, sibling)

    def compute(distance):
        chip = chip_at(lax.rem(place - distance + 2 * chips, chips), chips, two_columns)
        both = pl.ds(pl.multiple_of(chip * 2 * rows, 2 * rows), 2 * rows)
        total = dot_nt(grad[...], held[both, :]) + dot_nt(upstream_ref[...], down_ref[both, :])
        out_ref[chip] = total.astype(out_ref.dtype)

    load_weight.wait()
    for h in range(HALVES):
        forward(h, 0, me).start()
        backward(h, 0, me).start()
    mine = held.at[pl.ds(pl.multiple_of(me * rows, rows), rows)]
    twin = me + 1 - 2 * core
    twins = held.at[pl.ds(pl.multiple_of(twin * rows, rows), rows)]
    own = pltpu.make_async_remote_copy(
        src_ref=mine, dst_ref=mine, send_sem=own_send, recv_sem=own_recv,
        device_id=sibling, device_id_type=MESH,
    )
    own_in = pltpu.make_async_remote_copy(
        src_ref=twins, dst_ref=twins, send_sem=own_send, recv_sem=own_recv,
        device_id=sibling, device_id_type=MESH,
    )
    own.start()
    load_grad.wait()
    own_in.wait_recv()
    compute(0)

    def pass_cross(step):
        from_behind = device(place - 1 - step)
        for h in range(HALVES):
            cross_in(h, step, from_behind).wait_recv()
            share(2, h, step, from_behind, cut_far).start()

    def wait_shared(distance):
        owner = device(place - distance) + 1 - 2 * core
        step, step_back = distance - 1, chips - distance - 1
        for h in range(HALVES):
            share(0, h, step, owner, cut_near).wait_recv()
            share(2, h, step, owner, cut_far).wait_recv()
            share(1, h, step_back, owner, cut_mid).wait_recv()

    def step_body(step, carry):
        from_behind, from_ahead = device(place - 1 - step), device(place + 1 + step)
        for h in range(HALVES):
            forward(h, step, from_behind).wait_recv()

            @pl.when(step + 1 < steps)
            def _():
                forward(h, step + 1, from_behind).start()

            cross(h, step, from_behind).start()
            share(0, h, step, from_behind, cut_near).start()
            backward(h, step, from_ahead).wait_recv()

            @pl.when(step + 1 < steps)
            def _():
                backward(h, step + 1, from_ahead).start()

            share(1, h, step, from_ahead, cut_mid).start()

        @pl.when(step >= 1)
        def _():
            pass_cross(step - 1)

        @pl.when(step >= chips // 2)
        def _():
            def both(k, carry):
                distance = jnp.where(k == 0, step, chips - 1 - step)
                wait_shared(distance)
                compute(distance)
                return carry

            lax.fori_loop(0, 2, both, 0)

        return carry

    lax.fori_loop(0, steps, step_body, 0)
    pass_cross(steps - 1)
    wait_shared(steps)
    compute(steps)

    def drain(step, carry):
        from_behind, from_ahead = device(place - 1 - step), device(place + 1 + step)
        for h in range(HALVES):
            forward(h, step, from_behind).wait_send()
            backward(h, step, from_ahead).wait_send()
            cross(h, step, from_behind).wait_send()
            share(0, h, step, from_behind, cut_near).wait_send()
            share(1, h, step, from_ahead, cut_mid).wait_send()
            share(2, h, step, from_behind, cut_far).wait_send()
        return carry

    lax.fori_loop(0, steps, drain, 0)
    own.wait_send()


def dense_part(groups, output_gradient, frozen_weight, upstream, down_all):
    tokens, features = output_gradient.shape
    rows = frozen_weight.shape[0]
    devices = down_all.shape[0] // rows
    chips = devices // 2
    side = features // 128 // 3 * 128
    middle = features - 2 * side
    steps = chips - 1
    vmem = pl.BlockSpec(memory_space=pltpu.VMEM)
    hbm = pl.BlockSpec(memory_space=pl.ANY)
    blocks = pl.pallas_call(
        functools.partial(dense_kernel, chips, groups == 2, rows, features, side, middle),
        out_shape=jax.ShapeDtypeStruct((chips, tokens, 2 * rows), jnp.bfloat16),
        in_specs=[hbm, hbm, vmem, vmem],
        out_specs=vmem,
        scratch_shapes=[
            pltpu.VMEM((devices * rows, features), jnp.bfloat16),
            pltpu.VMEM((tokens, features), jnp.bfloat16),
            pltpu.SemaphoreType.DMA((2,)),
            pltpu.SemaphoreType.DMA((6, HALVES, steps)),
            pltpu.SemaphoreType.DMA((6, HALVES, steps)),
            pltpu.SemaphoreType.DMA,
            pltpu.SemaphoreType.DMA,
        ],
        compiler_params=pltpu.CompilerParams(
            collective_id=0, has_side_effects=True, vmem_limit_bytes=52 * 1024 * 1024
        ),
        cost_estimate=pl.CostEstimate(
            flops=2 * tokens * features * devices * rows * 10,
            bytes_accessed=2 * features * devices * rows * 6, transcendentals=0,
        ),
    )(output_gradient, frozen_weight, upstream, down_all)
    return jnp.transpose(blocks, (1, 0, 2)).reshape(tokens, devices * rows)


def shards(groups, layer_input, output_gradient, frozen_weight, adapter_down, adapter_up_matrix):
    devices = lax.axis_size("fsdp")
    objective_scale = 1.0 / math.sqrt(layer_input.shape[0] * devices)
    rows, rank = adapter_down.shape
    packed = jnp.concatenate([adapter_down, adapter_up_matrix.T], axis=0)
    packed = lax.all_gather(packed, "fsdp", axis=0)
    down_all = packed[:, :rows].reshape(-1, rank)
    up_all = packed[:, rows:].reshape(-1, rank)
    latent = jnp.dot(layer_input, down_all, preferred_element_type=jnp.float32).astype(
        jnp.bfloat16
    )
    upstream = (
        adapter_scale * jnp.dot(output_gradient, up_all, preferred_element_type=jnp.float32)
    ).astype(jnp.bfloat16)
    part_down = dot_tn(layer_input, upstream) * objective_scale
    part_up = dot_tn(output_gradient, latent) * (adapter_scale * objective_scale)
    parts = jnp.concatenate(
        [part_down.reshape(devices, rows, rank), part_up.reshape(devices, -1, rank)], axis=1
    )
    parts, upstream = lax.optimization_barrier((parts, upstream))
    summed = lax.psum_scatter(parts, "fsdp", scatter_dimension=0, tiled=False)
    grad_input = dense_part(groups, output_gradient, frozen_weight, upstream, down_all)
    return (grad_input, summed[:rows], summed[rows:].T)


def solution(mesh):
    in_specs = (
        P(("groups", "fsdp"), None),
        P(("groups", "fsdp"), None),
        P("fsdp", None),
        P(("groups", "fsdp"), None),
        P("groups", "fsdp"),
    )
    out_specs = (P(("groups", "fsdp"), None), P(("groups", "fsdp"), None), P("groups", "fsdp"))
    return jax.shard_map(
        functools.partial(shards, mesh.shape["groups"]),
        mesh=mesh, in_specs=in_specs, out_specs=out_specs, check_vma=False,
    )
```

```python
import functools
import math

import jax
import jax.numpy as jnp
from jax import lax
from jax.experimental import pallas as pl
from jax.experimental.pallas import tpu as pltpu
from jax.sharding import PartitionSpec as P

adapter_scale = 2.0
MESH = pl.DeviceIdType.MESH
HALVES = 2


def dot_nt(left, right):
    return lax.dot_general(
        left, right, (((1,), (1,)), ((), ())), preferred_element_type=jnp.float32
    )


def dot_tn(left, right):
    return lax.dot_general(
        left, right, (((0,), (0,)), ((), ())), preferred_element_type=jnp.float32
    )


def chip_at(position, chips, two_columns):
    if not two_columns:
        return position
    return jnp.where(
        position < chips // 2, 2 * position, 2 * (chips - 1 - position) + 1
    )


def place_of(chip, chips, two_columns):
    if not two_columns:
        return chip
    row, column = chip // 2, chip % 2
    return jnp.where(column == 0, row, chips - 1 - row)


def dense_kernel(
    chips, two_columns, rows, features, side, middle,
    grad_ref, weight_ref, upstream_ref, down_ref, out_ref,
    held, grad, local_sem, send_sem, recv_sem, own_send, own_recv,
):
    group, me = lax.axis_index("groups"), lax.axis_index("fsdp")
    core = lax.rem(me, 2)
    place = place_of(me // 2, chips, two_columns)
    role = lax.rem(group, 2)
    steps = chips - 1
    half = rows // HALVES

    def device(position):
        return chip_at(lax.rem(position + 2 * chips, chips), chips, two_columns) * 2 + core

    ahead, behind = (group, device(place + 1)), (group, device(place - 1))
    across = (group + 1 - 2 * role, me)
    sibling = (group, me + 1 - 2 * core)

    load_weight = pltpu.make_async_copy(
        weight_ref, held.at[pl.ds(pl.multiple_of(me * rows, rows), rows)], local_sem.at[0]
    )
    load_grad = pltpu.make_async_copy(grad_ref, grad, local_sem.at[1])
    load_weight.start()
    load_grad.start()

    barrier = pltpu.get_barrier_semaphore()
    for other in (ahead, behind, across, sibling):
        pl.semaphore_signal(barrier, inc=1, device_id=other, device_id_type=MESH)
    pl.semaphore_wait(barrier, 4)

    near = pl.multiple_of(role * (side + middle), 128)
    far = pl.multiple_of((1 - role) * (side + middle), 128)

    def block(owner, h, columns):
        return held.at[pl.ds(pl.multiple_of(owner * rows + h * half, half), half), columns]

    cut_near, cut_far, cut_mid = pl.ds(near, side), pl.ds(far, side), pl.ds(side, middle)

    def copy(kind, h, step, owner, columns, target):
        ref = block(owner, h, columns)
        return pltpu.make_async_remote_copy(
            src_ref=ref, dst_ref=ref,
            send_sem=send_sem.at[kind, h, step], recv_sem=recv_sem.at[kind, h, step],
            device_id=target, device_id_type=MESH,
        )

    def forward(h, step, owner):
        return copy(0, h, step, owner, cut_near, ahead)

    def backward(h, step, owner):
        return copy(1, h, step, owner, cut_mid, behind)

    def cross(h, step, owner):
        return copy(2, h, step, owner, cut_near, across)

    def cross_in(h, step, owner):
        return copy(2, h, step, owner, cut_far, across)

    def share(kind, h, step, owner, columns):
        return copy(3 + kind, h, step, owner, columns, sibling)

    def compute(distance):
        chip = chip_at(lax.rem(place - distance + 2 * chips, chips), chips, two_columns)
        both = pl.ds(pl.multiple_of(chip * 2 * rows, 2 * rows), 2 * rows)
        total = dot_nt(grad[...], held[both, :]) + dot_nt(upstream_ref[...], down_ref[both, :])
        if len(out_ref.shape) == 2:
            width = 2 * rows
            out_ref[:, pl.ds(pl.multiple_of(chip * width, width), width)] = total.astype(
                out_ref.dtype
            )
        else:
            out_ref[chip] = total.astype(out_ref.dtype)

    load_weight.wait()
    for h in range(HALVES):
        forward(h, 0, me).start()
        backward(h, 0, me).start()
    mine = held.at[pl.ds(pl.multiple_of(me * rows, rows), rows)]
    twin = me + 1 - 2 * core
    twins = held.at[pl.ds(pl.multiple_of(twin * rows, rows), rows)]
    own = pltpu.make_async_remote_copy(
        src_ref=mine, dst_ref=mine, send_sem=own_send, recv_sem=own_recv,
        device_id=sibling, device_id_type=MESH,
    )
    own_in = pltpu.make_async_remote_copy(
        src_ref=twins, dst_ref=twins, send_sem=own_send, recv_sem=own_recv,
        device_id=sibling, device_id_type=MESH,
    )
    own.start()
    load_grad.wait()
    own_in.wait_recv()
    compute(0)

    def pass_cross(step):
        from_behind = device(place - 1 - step)
        for h in range(HALVES):
            cross_in(h, step, from_behind).wait_recv()
            share(2, h, step, from_behind, cut_far).start()

    def wait_shared(distance):
        owner = device(place - distance) + 1 - 2 * core
        step, step_back = distance - 1, chips - distance - 1
        for h in range(HALVES):
            share(0, h, step, owner, cut_near).wait_recv()
            share(2, h, step, owner, cut_far).wait_recv()
            share(1, h, step_back, owner, cut_mid).wait_recv()

    def step_body(step, carry):
        from_behind, from_ahead = device(place - 1 - step), device(place + 1 + step)
        for h in range(HALVES):
            forward(h, step, from_behind).wait_recv()

            @pl.when(step + 1 < steps)
            def _():
                forward(h, step + 1, from_behind).start()

            cross(h, step, from_behind).start()
            share(0, h, step, from_behind, cut_near).start()
            backward(h, step, from_ahead).wait_recv()

            @pl.when(step + 1 < steps)
            def _():
                backward(h, step + 1, from_ahead).start()

            share(1, h, step, from_ahead, cut_mid).start()

        @pl.when(step >= 1)
        def _():
            pass_cross(step - 1)

        @pl.when(step >= chips // 2)
        def _():
            def both(k, carry):
                distance = jnp.where(k == 0, step, chips - 1 - step)
                wait_shared(distance)
                compute(distance)
                return carry

            lax.fori_loop(0, 2, both, 0)

        return carry

    lax.fori_loop(0, steps, step_body, 0)
    pass_cross(steps - 1)
    wait_shared(steps)
    compute(steps)

    def drain(step, carry):
        from_behind, from_ahead = device(place - 1 - step), device(place + 1 + step)
        for h in range(HALVES):
            forward(h, step, from_behind).wait_send()
            backward(h, step, from_ahead).wait_send()
            cross(h, step, from_behind).wait_send()
            share(0, h, step, from_behind, cut_near).wait_send()
            share(1, h, step, from_ahead, cut_mid).wait_send()
            share(2, h, step, from_behind, cut_far).wait_send()
        return carry

    lax.fori_loop(0, steps, drain, 0)
    own.wait_send()


def dense_part(groups, output_gradient, frozen_weight, upstream, down_all):
    tokens, features = output_gradient.shape
    rows = frozen_weight.shape[0]
    devices = down_all.shape[0] // rows
    chips = devices // 2
    side = features // 128 // 3 * 128
    middle = features - 2 * side
    steps = chips - 1
    vmem = pl.BlockSpec(memory_space=pltpu.VMEM)
    hbm = pl.BlockSpec(memory_space=pl.ANY)
    lanes = 2 * rows % 128 == 0
    shape = (tokens, devices * rows) if lanes else (chips, tokens, 2 * rows)
    blocks = pl.pallas_call(
        functools.partial(dense_kernel, chips, groups == 2, rows, features, side, middle),
        out_shape=jax.ShapeDtypeStruct(shape, jnp.bfloat16),
        in_specs=[hbm, hbm, vmem, vmem],
        out_specs=vmem,
        scratch_shapes=[
            pltpu.VMEM((devices * rows, features), jnp.bfloat16),
            pltpu.VMEM((tokens, features), jnp.bfloat16),
            pltpu.SemaphoreType.DMA((2,)),
            pltpu.SemaphoreType.DMA((6, HALVES, steps)),
            pltpu.SemaphoreType.DMA((6, HALVES, steps)),
            pltpu.SemaphoreType.DMA,
            pltpu.SemaphoreType.DMA,
        ],
        compiler_params=pltpu.CompilerParams(
            collective_id=0, has_side_effects=True, vmem_limit_bytes=52 * 1024 * 1024
        ),
        cost_estimate=pl.CostEstimate(
            flops=2 * tokens * features * devices * rows * 10,
            bytes_accessed=2 * features * devices * rows * 6, transcendentals=0,
        ),
    )(output_gradient, frozen_weight, upstream, down_all)
    if lanes:
        return blocks
    return jnp.transpose(blocks, (1, 0, 2)).reshape(tokens, devices * rows)


def gather_kernel(chips, two_columns, mine_ref, out_ref, send_sem, recv_sem, own_sem, local_sem):
    group, me = lax.axis_index("groups"), lax.axis_index("fsdp")
    core = lax.rem(me, 2)
    place = place_of(me // 2, chips, two_columns)
    forward_steps, backward_steps = chips // 2, chips - 1 - chips // 2

    def device(position):
        return chip_at(lax.rem(position + 2 * chips, chips), chips, two_columns) * 2 + core

    ahead, behind = (group, device(place + 1)), (group, device(place - 1))
    twin = me + 1 - 2 * core
    sibling = (group, twin)

    keep = pltpu.make_async_copy(mine_ref, out_ref.at[me], local_sem)
    keep.start()
    barrier = pltpu.get_barrier_semaphore()
    for other in (ahead, behind, sibling):
        pl.semaphore_signal(barrier, inc=1, device_id=other, device_id_type=MESH)
    pl.semaphore_wait(barrier, 3)
    keep.wait()

    def copy(kind, step, owner, target):
        return pltpu.make_async_remote_copy(
            src_ref=out_ref.at[owner], dst_ref=out_ref.at[owner],
            send_sem=send_sem.at[kind, step], recv_sem=recv_sem.at[kind, step],
            device_id=target, device_id_type=MESH,
        )

    def own(owner):
        return pltpu.make_async_remote_copy(
            src_ref=out_ref.at[owner], dst_ref=out_ref.at[owner],
            send_sem=own_sem.at[0], recv_sem=own_sem.at[1],
            device_id=sibling, device_id_type=MESH,
        )

    copy(0, 0, me, ahead).start()
    copy(1, 0, me, behind).start()
    own(me).start()

    def step_body(step, carry):
        from_behind, from_ahead = device(place - 1 - step), device(place + 1 + step)
        copy(0, step, from_behind, ahead).wait_recv()

        @pl.when(step + 1 < forward_steps)
        def _():
            copy(0, step + 1, from_behind, ahead).start()

        copy(2, step, from_behind, sibling).start()

        @pl.when(step < backward_steps)
        def _():
            copy(1, step, from_ahead, behind).wait_recv()

            @pl.when(step + 1 < backward_steps)
            def _():
                copy(1, step + 1, from_ahead, behind).start()

            copy(3, step, from_ahead, sibling).start()

        return carry

    lax.fori_loop(0, forward_steps, step_body, 0)

    def drain(step, carry):
        from_behind, from_ahead = device(place - 1 - step), device(place + 1 + step)
        swap = 1 - 2 * core
        copy(0, step, from_behind, ahead).wait_send()
        copy(2, step, from_behind, sibling).wait_send()
        copy(2, step, from_behind + swap, sibling).wait_recv()

        @pl.when(step < backward_steps)
        def _():
            copy(1, step, from_ahead, behind).wait_send()
            copy(3, step, from_ahead, sibling).wait_send()
            copy(3, step, from_ahead + swap, sibling).wait_recv()

        return carry

    lax.fori_loop(0, forward_steps, drain, 0)
    own(me).wait_send()
    own(twin).wait_recv()


def gather_small(groups, devices, packed):
    chips = devices // 2
    vmem = pl.BlockSpec(memory_space=pltpu.VMEM)
    return pl.pallas_call(
        functools.partial(gather_kernel, chips, groups == 2),
        out_shape=jax.ShapeDtypeStruct((devices, *packed.shape), packed.dtype),
        in_specs=[vmem],
        out_specs=vmem,
        scratch_shapes=[
            pltpu.SemaphoreType.DMA((4, chips // 2)),
            pltpu.SemaphoreType.DMA((4, chips // 2)),
            pltpu.SemaphoreType.DMA((2,)),
            pltpu.SemaphoreType.DMA,
        ],
        compiler_params=pltpu.CompilerParams(
            collective_id=1, has_side_effects=True, vmem_limit_bytes=16 * 1024 * 1024
        ),
    )(packed)


def shards(groups, layer_input, output_gradient, frozen_weight, adapter_down, adapter_up_matrix):
    devices = lax.axis_size("fsdp")
    objective_scale = 1.0 / math.sqrt(layer_input.shape[0] * devices)
    rows, rank = adapter_down.shape
    width = adapter_up_matrix.shape[1]
    packed = jnp.concatenate([adapter_down.T, adapter_up_matrix], axis=1)
    packed = jnp.pad(packed, ((0, 0), (0, -(rows + width) % 128)))
    packed = gather_small(groups, devices, packed)
    down_all = jnp.transpose(packed[:, :, :rows], (0, 2, 1)).reshape(-1, rank)
    up_all = jnp.transpose(packed[:, :, rows : rows + width], (0, 2, 1)).reshape(-1, rank)
    latent = jnp.dot(layer_input, down_all, preferred_element_type=jnp.float32).astype(
        jnp.bfloat16
    )
    upstream = (
        adapter_scale * jnp.dot(output_gradient, up_all, preferred_element_type=jnp.float32)
    ).astype(jnp.bfloat16)
    part_down = dot_tn(layer_input, upstream) * objective_scale
    part_up = dot_tn(output_gradient, latent) * (adapter_scale * objective_scale)
    parts = jnp.concatenate(
        [part_down.reshape(devices, rows, rank), part_up.reshape(devices, -1, rank)], axis=1
    )
    parts, upstream = lax.optimization_barrier((parts, upstream))
    summed = lax.psum_scatter(parts, "fsdp", scatter_dimension=0, tiled=False)
    grad_input = dense_part(groups, output_gradient, frozen_weight, upstream, down_all)
    return (grad_input, summed[:rows], summed[rows:].T)


def solution(mesh):
    in_specs = (
        P(("groups", "fsdp"), None),
        P(("groups", "fsdp"), None),
        P("fsdp", None),
        P(("groups", "fsdp"), None),
        P("groups", "fsdp"),
    )
    out_specs = (P(("groups", "fsdp"), None), P(("groups", "fsdp"), None), P("groups", "fsdp"))
    return jax.shard_map(
        functools.partial(shards, mesh.shape["groups"]),
        mesh=mesh, in_specs=in_specs, out_specs=out_specs, check_vma=False,
    )
```

```python
import functools
import math

import jax
import jax.numpy as jnp
from jax import lax
from jax.experimental import pallas as pl
from jax.experimental.pallas import tpu as pltpu
from jax.sharding import PartitionSpec as P

adapter_scale = 2.0
MESH = pl.DeviceIdType.MESH
HALVES = 2
EARLY = 2


def dot_nt(left, right):
    return lax.dot_general(
        left, right, (((1,), (1,)), ((), ())), preferred_element_type=jnp.float32
    )


def dot_tn(left, right):
    return lax.dot_general(
        left, right, (((0,), (0,)), ((), ())), preferred_element_type=jnp.float32
    )


def chip_at(position, chips, two_columns):
    if not two_columns:
        return position
    return jnp.where(
        position < chips // 2, 2 * position, 2 * (chips - 1 - position) + 1
    )


def place_of(chip, chips, two_columns):
    if not two_columns:
        return chip
    row, column = chip // 2, chip % 2
    return jnp.where(column == 0, row, chips - 1 - row)


def dense_kernel(
    chips, two_columns, rows, features, side, middle,
    grad_ref, weight_ref, upstream_ref, down_ref,
    ahead_one, ahead_two, behind_one, behind_two, across_one, out_ref,
    held, grad, local_sem, send_sem, recv_sem, own_send, own_recv,
):
    group, me = lax.axis_index("groups"), lax.axis_index("fsdp")
    core = lax.rem(me, 2)
    place = place_of(me // 2, chips, two_columns)
    role = lax.rem(group, 2)
    steps = chips - 1
    half = rows // HALVES

    def device(position):
        return chip_at(lax.rem(position + 2 * chips, chips), chips, two_columns) * 2 + core

    ahead, behind = (group, device(place + 1)), (group, device(place - 1))
    across = (group + 1 - 2 * role, me)
    sibling = (group, me + 1 - 2 * core)

    load_weight = pltpu.make_async_copy(
        weight_ref, held.at[pl.ds(pl.multiple_of(me * rows, rows), rows)], local_sem.at[0]
    )
    load_grad = pltpu.make_async_copy(grad_ref, grad, local_sem.at[1])
    load_weight.start()
    load_grad.start()
    first, second = pl.ds(side, middle), pl.ds(pl.multiple_of(role * (side + middle), 128), side)
    other = pl.ds(pl.multiple_of((1 - role) * (side + middle), 128), side)
    early = []
    for k, (ref, distance, columns) in enumerate((
        (ahead_one, -1, second), (ahead_two, -2, second), (behind_one, 1, first),
        (behind_two, 2, first), (across_one, -1, other),
    )):
        owner = device(place + distance)
        early.append(pltpu.make_async_copy(
            ref, held.at[pl.ds(pl.multiple_of(owner * rows, rows), rows), columns],
            local_sem.at[2 + k],
        ))
        early[-1].start()

    barrier = pltpu.get_barrier_semaphore()
    for other in (ahead, behind, across, sibling):
        pl.semaphore_signal(barrier, inc=1, device_id=other, device_id_type=MESH)
    pl.semaphore_wait(barrier, 4)

    near = pl.multiple_of(role * (side + middle), 128)
    far = pl.multiple_of((1 - role) * (side + middle), 128)

    def block(owner, h, columns):
        return held.at[pl.ds(pl.multiple_of(owner * rows + h * half, half), half), columns]

    cut_near, cut_far, cut_mid = pl.ds(near, side), pl.ds(far, side), pl.ds(side, middle)

    def copy(kind, h, step, owner, columns, target):
        ref = block(owner, h, columns)
        return pltpu.make_async_remote_copy(
            src_ref=ref, dst_ref=ref,
            send_sem=send_sem.at[kind, h, step], recv_sem=recv_sem.at[kind, h, step],
            device_id=target, device_id_type=MESH,
        )

    def forward(h, step, owner):
        return copy(0, h, step, owner, cut_near, ahead)

    def backward(h, step, owner):
        return copy(1, h, step, owner, cut_mid, behind)

    def cross(h, step, owner):
        return copy(2, h, step, owner, cut_near, across)

    def cross_in(h, step, owner):
        return copy(2, h, step, owner, cut_far, across)

    def share(kind, h, step, owner, columns):
        return copy(3 + kind, h, step, owner, columns, sibling)

    def compute(distance):
        chip = chip_at(lax.rem(place - distance + 2 * chips, chips), chips, two_columns)
        both = pl.ds(pl.multiple_of(chip * 2 * rows, 2 * rows), 2 * rows)
        total = dot_nt(grad[...], held[both, :]) + dot_nt(upstream_ref[...], down_ref[both, :])
        if len(out_ref.shape) == 2:
            width = 2 * rows
            out_ref[:, pl.ds(pl.multiple_of(chip * width, width), width)] = total.astype(
                out_ref.dtype
            )
        else:
            out_ref[chip] = total.astype(out_ref.dtype)

    load_weight.wait()
    for load in early:
        load.wait()
    for h in range(HALVES):
        forward(h, EARLY, device(place - EARLY)).start()
        backward(h, EARLY, device(place + EARLY)).start()
        cross(h, EARLY - 1, device(place - EARLY)).start()
    mine = held.at[pl.ds(pl.multiple_of(me * rows, rows), rows)]
    twin = me + 1 - 2 * core
    twins = held.at[pl.ds(pl.multiple_of(twin * rows, rows), rows)]
    own = pltpu.make_async_remote_copy(
        src_ref=mine, dst_ref=mine, send_sem=own_send, recv_sem=own_recv,
        device_id=sibling, device_id_type=MESH,
    )
    own_in = pltpu.make_async_remote_copy(
        src_ref=twins, dst_ref=twins, send_sem=own_send, recv_sem=own_recv,
        device_id=sibling, device_id_type=MESH,
    )
    own.start()
    load_grad.wait()
    own_in.wait_recv()
    compute(0)

    def pass_cross(step):
        from_behind = device(place - 1 - step)
        for h in range(HALVES):
            cross_in(h, step, from_behind).wait_recv()
            share(2, h, step, from_behind, cut_far).start()

    for h in range(HALVES):
        for step in range(EARLY):
            share(0, h, step, device(place - 1 - step), cut_near).start()
            share(1, h, step, device(place + 1 + step), cut_mid).start()
        share(2, h, 0, device(place - 1), cut_far).start()

    def wait_shared(distance):
        owner = device(place - distance) + 1 - 2 * core
        step, step_back = distance - 1, chips - distance - 1
        for h in range(HALVES):
            share(0, h, step, owner, cut_near).wait_recv()
            share(2, h, step, owner, cut_far).wait_recv()
            share(1, h, step_back, owner, cut_mid).wait_recv()

    def step_body(step, carry):
        from_behind, from_ahead = device(place - 1 - step), device(place + 1 + step)
        for h in range(HALVES):
            forward(h, step, from_behind).wait_recv()

            @pl.when(step + 1 < steps)
            def _():
                forward(h, step + 1, from_behind).start()

            cross(h, step, from_behind).start()
            share(0, h, step, from_behind, cut_near).start()
            backward(h, step, from_ahead).wait_recv()

            @pl.when(step + 1 < steps)
            def _():
                backward(h, step + 1, from_ahead).start()

            share(1, h, step, from_ahead, cut_mid).start()

        pass_cross(step - 1)

        @pl.when(step >= chips // 2)
        def _():
            def both(k, carry):
                distance = jnp.where(k == 0, step, chips - 1 - step)
                wait_shared(distance)
                compute(distance)
                return carry

            lax.fori_loop(0, 2, both, 0)

        return carry

    lax.fori_loop(EARLY, steps, step_body, 0)
    pass_cross(steps - 1)
    wait_shared(steps)
    compute(steps)

    def drain(step, carry):
        from_behind, from_ahead = device(place - 1 - step), device(place + 1 + step)
        for h in range(HALVES):
            share(0, h, step, from_behind, cut_near).wait_send()
            share(1, h, step, from_ahead, cut_mid).wait_send()
            share(2, h, step, from_behind, cut_far).wait_send()

            @pl.when(step >= EARLY)
            def _():
                forward(h, step, from_behind).wait_send()
                backward(h, step, from_ahead).wait_send()

            @pl.when(step >= EARLY - 1)
            def _():
                cross(h, step, from_behind).wait_send()
        return carry

    lax.fori_loop(0, steps, drain, 0)
    own.wait_send()


def early_hops(groups, devices, frozen_weight):
    chips = devices // 2
    features = frozen_weight.shape[1]
    side = features // 128 // 3 * 128
    middle = features - 2 * side
    ring = list(range(chips))
    if groups == 2:
        ring = list(range(0, chips, 2)) + list(range(chips - 1, 0, -2))
    onward = [
        (ring[k] * 2 + core, ring[(k + 1) % chips] * 2 + core)
        for k in range(chips) for core in range(2)
    ]
    back = [(target, source) for source, target in onward]
    role = lax.rem(lax.axis_index("groups"), 2)
    near = jnp.where(role == 0, frozen_weight[:, :side], frozen_weight[:, side + middle :])
    mid = frozen_weight[:, side : side + middle]
    ahead_one = lax.ppermute(near, "fsdp", onward)
    behind_one = lax.ppermute(mid, "fsdp", back)
    across_one = lax.ppermute(ahead_one, "groups", [(g, g ^ 1) for g in range(groups)])
    ahead_two = lax.ppermute(ahead_one, "fsdp", onward)
    behind_two = lax.ppermute(behind_one, "fsdp", back)
    return ahead_one, ahead_two, behind_one, behind_two, across_one


def dense_part(groups, output_gradient, frozen_weight, upstream, down_all, early):
    tokens, features = output_gradient.shape
    rows = frozen_weight.shape[0]
    devices = down_all.shape[0] // rows
    chips = devices // 2
    side = features // 128 // 3 * 128
    middle = features - 2 * side
    steps = chips - 1
    vmem = pl.BlockSpec(memory_space=pltpu.VMEM)
    hbm = pl.BlockSpec(memory_space=pl.ANY)
    lanes = 2 * rows % 128 == 0
    shape = (tokens, devices * rows) if lanes else (chips, tokens, 2 * rows)
    blocks = pl.pallas_call(
        functools.partial(dense_kernel, chips, groups == 2, rows, features, side, middle),
        out_shape=jax.ShapeDtypeStruct(shape, jnp.bfloat16),
        in_specs=[hbm, hbm, vmem, vmem] + [hbm] * 5,
        out_specs=vmem,
        scratch_shapes=[
            pltpu.VMEM((devices * rows, features), jnp.bfloat16),
            pltpu.VMEM((tokens, features), jnp.bfloat16),
            pltpu.SemaphoreType.DMA((7,)),
            pltpu.SemaphoreType.DMA((6, HALVES, steps)),
            pltpu.SemaphoreType.DMA((6, HALVES, steps)),
            pltpu.SemaphoreType.DMA,
            pltpu.SemaphoreType.DMA,
        ],
        compiler_params=pltpu.CompilerParams(
            collective_id=0, has_side_effects=True, vmem_limit_bytes=52 * 1024 * 1024
        ),
        cost_estimate=pl.CostEstimate(
            flops=2 * tokens * features * devices * rows * 10,
            bytes_accessed=2 * features * devices * rows * 6, transcendentals=0,
        ),
    )(output_gradient, frozen_weight, upstream, down_all, *early)
    if lanes:
        return blocks
    return jnp.transpose(blocks, (1, 0, 2)).reshape(tokens, devices * rows)


def gather_kernel(chips, two_columns, mine_ref, out_ref, send_sem, recv_sem, own_sem, local_sem):
    group, me = lax.axis_index("groups"), lax.axis_index("fsdp")
    core = lax.rem(me, 2)
    place = place_of(me // 2, chips, two_columns)
    forward_steps, backward_steps = chips // 2, chips - 1 - chips // 2

    def device(position):
        return chip_at(lax.rem(position + 2 * chips, chips), chips, two_columns) * 2 + core

    ahead, behind = (group, device(place + 1)), (group, device(place - 1))
    twin = me + 1 - 2 * core
    sibling = (group, twin)

    keep = pltpu.make_async_copy(mine_ref, out_ref.at[me], local_sem)
    keep.start()
    barrier = pltpu.get_barrier_semaphore()
    for other in (ahead, behind, sibling):
        pl.semaphore_signal(barrier, inc=1, device_id=other, device_id_type=MESH)
    pl.semaphore_wait(barrier, 3)
    keep.wait()

    def copy(kind, step, owner, target):
        return pltpu.make_async_remote_copy(
            src_ref=out_ref.at[owner], dst_ref=out_ref.at[owner],
            send_sem=send_sem.at[kind, step], recv_sem=recv_sem.at[kind, step],
            device_id=target, device_id_type=MESH,
        )

    def own(owner):
        return pltpu.make_async_remote_copy(
            src_ref=out_ref.at[owner], dst_ref=out_ref.at[owner],
            send_sem=own_sem.at[0], recv_sem=own_sem.at[1],
            device_id=sibling, device_id_type=MESH,
        )

    copy(0, 0, me, ahead).start()
    copy(1, 0, me, behind).start()
    own(me).start()

    def step_body(step, carry):
        from_behind, from_ahead = device(place - 1 - step), device(place + 1 + step)
        copy(0, step, from_behind, ahead).wait_recv()

        @pl.when(step + 1 < forward_steps)
        def _():
            copy(0, step + 1, from_behind, ahead).start()

        copy(2, step, from_behind, sibling).start()

        @pl.when(step < backward_steps)
        def _():
            copy(1, step, from_ahead, behind).wait_recv()

            @pl.when(step + 1 < backward_steps)
            def _():
                copy(1, step + 1, from_ahead, behind).start()

            copy(3, step, from_ahead, sibling).start()

        return carry

    lax.fori_loop(0, forward_steps, step_body, 0)

    def drain(step, carry):
        from_behind, from_ahead = device(place - 1 - step), device(place + 1 + step)
        swap = 1 - 2 * core
        copy(0, step, from_behind, ahead).wait_send()
        copy(2, step, from_behind, sibling).wait_send()
        copy(2, step, from_behind + swap, sibling).wait_recv()

        @pl.when(step < backward_steps)
        def _():
            copy(1, step, from_ahead, behind).wait_send()
            copy(3, step, from_ahead, sibling).wait_send()
            copy(3, step, from_ahead + swap, sibling).wait_recv()

        return carry

    lax.fori_loop(0, forward_steps, drain, 0)
    own(me).wait_send()
    own(twin).wait_recv()


def gather_small(groups, devices, packed):
    chips = devices // 2
    vmem = pl.BlockSpec(memory_space=pltpu.VMEM)
    return pl.pallas_call(
        functools.partial(gather_kernel, chips, groups == 2),
        out_shape=jax.ShapeDtypeStruct((devices, *packed.shape), packed.dtype),
        in_specs=[vmem],
        out_specs=vmem,
        scratch_shapes=[
            pltpu.SemaphoreType.DMA((4, chips // 2)),
            pltpu.SemaphoreType.DMA((4, chips // 2)),
            pltpu.SemaphoreType.DMA((2,)),
            pltpu.SemaphoreType.DMA,
        ],
        compiler_params=pltpu.CompilerParams(
            collective_id=1, has_side_effects=True, vmem_limit_bytes=16 * 1024 * 1024
        ),
        cost_estimate=pl.CostEstimate(
            flops=0, bytes_accessed=40 * 1024 * 1024, transcendentals=0
        ),
    )(packed)


def shards(groups, layer_input, output_gradient, frozen_weight, adapter_down, adapter_up_matrix):
    devices = lax.axis_size("fsdp")
    objective_scale = 1.0 / math.sqrt(layer_input.shape[0] * devices)
    rows, rank = adapter_down.shape
    width = adapter_up_matrix.shape[1]
    packed = jnp.concatenate([adapter_down.T, adapter_up_matrix], axis=1)
    packed = jnp.pad(packed, ((0, 0), (0, -(rows + width) % 128)))
    early = early_hops(groups, devices, frozen_weight)
    packed = gather_small(groups, devices, packed)
    down_all = jnp.transpose(packed[:, :, :rows], (0, 2, 1)).reshape(-1, rank)
    up_all = jnp.transpose(packed[:, :, rows : rows + width], (0, 2, 1)).reshape(-1, rank)
    latent = jnp.dot(layer_input, down_all, preferred_element_type=jnp.float32).astype(
        jnp.bfloat16
    )
    upstream = (
        adapter_scale * jnp.dot(output_gradient, up_all, preferred_element_type=jnp.float32)
    ).astype(jnp.bfloat16)
    part_down = dot_tn(layer_input, upstream) * objective_scale
    part_up = dot_tn(output_gradient, latent) * (adapter_scale * objective_scale)
    parts = jnp.concatenate(
        [part_down.reshape(devices, rows, rank), part_up.reshape(devices, -1, rank)], axis=1
    )
    parts, upstream = lax.optimization_barrier((parts, upstream))
    summed = lax.psum_scatter(parts, "fsdp", scatter_dimension=0, tiled=False)
    grad_input = dense_part(
        groups, output_gradient, frozen_weight, upstream, down_all, early
    )
    return (grad_input, summed[:rows], summed[rows:].T)


def solution(mesh):
    in_specs = (
        P(("groups", "fsdp"), None),
        P(("groups", "fsdp"), None),
        P("fsdp", None),
        P(("groups", "fsdp"), None),
        P("groups", "fsdp"),
    )
    out_specs = (P(("groups", "fsdp"), None), P(("groups", "fsdp"), None), P("groups", "fsdp"))
    return jax.shard_map(
        functools.partial(shards, mesh.shape["groups"]),
        mesh=mesh, in_specs=in_specs, out_specs=out_specs, check_vma=False,
    )
```
